512 devices in a mesh: row: 32 (over z_lo, y, core), col: 16 (over x, z_hi).
Axes of the slice: x: 4, y: 8, z: 8 (z_hi: 4, z_lo: 2; z = z_hi * 2 + z_lo), core: 2. Of those that a mesh axis runs over, the one named last changes fastest.
Arguments:
- pair: bfloat16 [512, 512, 128], P('row', 'col'), may hold values from -6 to 6
- pair_mask: int32 [512, 512], P('row', 'col'), may hold values 0 or 1
- gain_in: float32 [128], replicated, may hold values from 0.1 to 1.9
- w_in: bfloat16 [128, 512], replicated, may hold values from -0.5 to 0.5
- w_gate: bfloat16 [128, 128], replicated, may hold values from -0.5 to 0.5
- gain_mid: float32 [128], replicated, may hold values from 0.1 to 1.9
- w_out: bfloat16 [128, 128], replicated, may hold values from -0.5 to 0.5
Outputs:
- pair_out: bfloat16 [512, 512, 128], P('row', 'col')
The draws below stay inside these ranges and needn't reach their ends.
All inputs are finite; a program needn't handle non-finite values. No bound on the sum of `pair_mask` on one device may be relied on, other than what follows from the above.
Results may differ from the reference program's by a relative error of at most 0.013.
Values may be sent and summed in bfloat16 or wider, within the bound.
No kernel may reach another device: no remote copies, remote signals or barrier semaphores. Data moves between devices by JAX's collectives and lax.ppermute only.
A program may use at most 64 MiB of HBM per device.

```python
import jax
import jax.numpy as jnp
from jax import lax

C = 128
NT = 512


def set_ends(drawn, rng, least, high):
    index_at = [jax.random.randint(jax.random.fold_in(rng, axis), (), 0, length) for axis, length in enumerate(drawn.shape)]
    main_axis = drawn.shape.index(max(drawn.shape))
    next_to = index_at[:main_axis] + [(index_at[main_axis] + 1) % drawn.shape[main_axis]] + index_at[main_axis + 1:]
    return drawn.at[tuple(index_at)].set(least).at[tuple(next_to)].set(high)


def level_of(own_key, extent, cuts, low, high):
    gain, own = 1.0, jax.random.fold_in(own_key, 6)
    for position, blocks in cuts:
        steps = jnp.exp(jax.random.uniform(jax.random.fold_in(own, position), (blocks,), jnp.float32, low / len(cuts), high / len(cuts)))
        gain = gain * jnp.repeat(steps, extent[position] // blocks).reshape([-1 if axis == position else 1 for axis in range(len(extent))])
    return gain


def scatter_about(key, dims, scale, most, split=(), dtype=jnp.bfloat16):
    array = scale * jax.random.normal(key, dims, jnp.float32)
    if split:
        array = array * level_of(key, dims, split, -0.22, 0.18)
    return jnp.clip(array, -most, most).astype(dtype)


def setup_inputs(seed: int = 0) -> dict:
    streams_of = jax.random.split(jax.random.key(seed), 8)
    return {
        "pair": scatter_about(streams_of[0], (NT, NT, C), 1.0, 6.0, ((0, 32), (1, 16))),
        "pair_mask": set_ends((jax.random.randint(streams_of[1], (NT, NT), 0, 16) < 15).astype(jnp.int32), jax.random.fold_in(streams_of[1], 1), 0, 1),
        "gain_in": jnp.clip(1.0 + 0.18 * jax.random.normal(streams_of[2], (C,), jnp.float32), 0.1, 1.9),
        "w_in": scatter_about(streams_of[3], (C, 4 * C), C ** -0.5, 0.5),
        "w_gate": scatter_about(streams_of[4], (C, C), C ** -0.5, 0.5),
        "gain_mid": jnp.clip(1.0 + 0.18 * jax.random.normal(streams_of[5], (C,), jnp.float32), 0.1, 1.9),
        "w_out": scatter_about(streams_of[6], (C, C), C ** -0.5, 0.5),
    }


def layer_norm(values, scale):
    center = values - lax.optimization_barrier(jnp.mean(values, axis=-1, keepdims=True))
    spread = lax.optimization_barrier(jnp.mean(center * center, axis=-1, keepdims=True))
    return center * lax.rsqrt(spread + 1e-05) * scale

def triangle_inputs(pair, pair_mask, gain_in, w_in):
    width = pair.shape[-1]
    normed = layer_norm(pair.astype(jnp.float32), gain_in).astype(jnp.bfloat16)
    projected = jnp.dot(normed.reshape(-1, width), w_in, preferred_element_type=jnp.float32)
    projected = projected.reshape(pair.shape[0], pair.shape[1], 4 * width)
    keeper = pair_mask.astype(jnp.float32)[:, :, None]
    left_side = jax.nn.sigmoid(projected[..., :width]) * projected[..., width:2 * width] * keeper
    right_side = jax.nn.sigmoid(projected[..., 2 * width:3 * width]) * projected[..., 3 * width:] * keeper
    return (normed, left_side.astype(jnp.bfloat16), right_side.astype(jnp.bfloat16))

def triangle_output(pair, normed, summed, gain_mid, w_gate, w_out):
    width = pair.shape[-1]
    gating = jax.nn.sigmoid(jnp.dot(normed.reshape(-1, width), w_gate, preferred_element_type=jnp.float32))
    middle = layer_norm(summed, gain_mid).astype(jnp.bfloat16).reshape(-1, width)
    update = gating * jnp.dot(middle, w_out, preferred_element_type=jnp.float32)
    result = pair.astype(jnp.float32).reshape(-1, width) + update
    return result.reshape(pair.shape).astype(jnp.bfloat16)

def reference(pair, pair_mask, gain_in, w_in, w_gate, gain_mid, w_out):
    normed, left_side, right_side = triangle_inputs(pair, pair_mask, gain_in, w_in)
    summed = jnp.einsum('ikc,jkc->ijc', left_side.astype(jnp.float32), right_side.astype(jnp.float32))
    return triangle_output(pair, normed, summed, gain_mid, w_gate, w_out)
```

```python
import jax
import jax.numpy as jnp
from jax import lax
from jax.experimental import pallas as pl
from jax.experimental.pallas import tpu as pltpu
from jax.sharding import Mesh
from jax.sharding import PartitionSpec as P

AXES = ("z_lo", "y", "core", "x", "z_hi")
ORDER = ("x", "z_hi", "core", "z_lo", "y")
F32, BF16 = jnp.float32, jnp.bfloat16


def iota(shape, axis):
    return lax.broadcasted_iota(jnp.int32, shape, axis)


def project(pair_ref, mask_ref, gain_ref, w_in_ref, w_gate_ref, send_ref, gate_ref):
    values = pair_ref[...].astype(F32)
    center = values - jnp.mean(values, axis=-1, keepdims=True)
    spread = jnp.mean(center * center, axis=-1, keepdims=True)
    normed = (center * lax.rsqrt(spread + 1e-05) * gain_ref[...]).astype(BF16)
    gate_ref[...] = jax.nn.sigmoid(jnp.dot(normed, w_gate_ref[...], preferred_element_type=F32))
    tokens = jnp.concatenate(
        [
            normed[core * 256 + i * 32 + half * 16 :][:16]
            for core in range(2)
            for half in range(2)
            for i in range(8)
        ],
        axis=0,
    )
    place = iota((32, 512), 1)
    column = (place >> 7 & 1) * 16 + (place & 15)
    spread_mask = jnp.dot(
        mask_ref[...].astype(F32), (column == iota((32, 512), 0)).astype(F32), preferred_element_type=F32
    )
    place = iota((16, 512), 1)
    row = (place >> 8) * 8 + (place >> 4 & 7)
    keeper = jnp.sum(jnp.where(row == iota((16, 512), 0), spread_mask, 0.0), axis=0, keepdims=True)
    projected = lax.dot_general(w_in_ref[...], tokens, (((0,), (1,)), ((), ())), preferred_element_type=F32)
    for side in range(2):
        start = side * 256
        both = (
            jax.nn.sigmoid(projected[start : start + 128]) * projected[start + 128 : start + 256] * keeper
        )
        for q in range(16):
            block = both[q * 8 : q * 8 + 8]
            for core in range(2):
                two = jnp.concatenate(
                    [block[:, core * 256 : core * 256 + 128], block[:, core * 256 + 128 : core * 256 + 256]], axis=0
                )
                send_ref[q * 32 + core * 16 : q * 32 + core * 16 + 16, side * 128 : side * 128 + 128] = two.astype(BF16)


def assemble(got_ref, left_ref, right_ref):
    for i in range(8):
        left_ref[i * 32 : i * 32 + 32, :] = jnp.concatenate(
            [got_ref[q * 32 : q * 32 + 32, i * 16 : i * 16 + 16] for q in range(16)], axis=1
        )
    right = jnp.concatenate(
        [
            jnp.concatenate(
                [got_ref[q * 32 : q * 32 + 32, 128 + j * 16 : 128 + j * 16 + 16] for q in range(16)], axis=1
            )
            for j in range(8)
        ],
        axis=0,
    )
    to, source = iota((256, 256), 0), iota((256, 256), 1)
    moved = ((to & 7) * 32 + (to >> 3 & 1) * 16 + (to >> 4)) == source
    right_ref[...] = jnp.dot(moved.astype(BF16), right, preferred_element_type=F32).astype(BF16)


def multiply(left_ref, right_ref, send_ref):
    summed = lax.dot_general(
        left_ref[...], right_ref[...], (((1,), (1,)), ((), ())), preferred_element_type=F32
    ).astype(BF16)
    for q in range(16):
        send_ref[q * 32 : q * 32 + 32, :] = jnp.concatenate(
            [summed[i * 32 : i * 32 + 32, q * 16 : q * 16 + 16] for i in range(16)], axis=1
        )


def finish(got_ref, pair_ref, gate_ref, gain_ref, w_out_ref, out_ref):
    same = iota((128, 128), 0) == iota((128, 128), 1)
    gain = jnp.sum(jnp.where(same, gain_ref[...], 0.0), axis=1, keepdims=True)
    updates = []
    for core in range(2):
        parts = []
        for q in range(16):
            two = got_ref[q * 32 + core * 16 : q * 32 + core * 16 + 16, :].astype(F32)
            parts.append(two[:8] + two[8:])
        summed = jnp.concatenate(parts, axis=0)
        center = summed - jnp.mean(summed, axis=0, keepdims=True)
        spread = jnp.mean(center * center, axis=0, keepdims=True)
        middle = (center * lax.rsqrt(spread + 1e-05) * gain).astype(BF16)
        updates.append(
            lax.dot_general(middle, w_out_ref[...], (((0,), (0,)), ((), ())), preferred_element_type=F32)
        )
    update = jnp.concatenate(
        [updates[core][at * 8 : at * 8 + 8] for at in range(32) for core in range(2)], axis=0
    )
    out_ref[...] = (pair_ref[...].astype(F32) + gate_ref[...] * update).astype(BF16)


def kernel(body, out_shape):
    return pl.pallas_call(
        body, out_shape=out_shape, compiler_params=pltpu.CompilerParams(vmem_limit_bytes=32 * 1024 * 1024)
    )


def exchange(rows):
    return lax.all_to_all(rows.reshape(512, 2, 128), ORDER, 0, 0).reshape(512, 256)


def shards(pair, pair_mask, gain_in, w_in, w_gate, gain_mid, w_out):
    tokens = pair.reshape(512, 128)
    array = jax.ShapeDtypeStruct
    sides, gate = kernel(project, (array((512, 256), BF16), array((512, 128), F32)))(
        tokens, pair_mask, gain_in.reshape(1, 128), w_in, w_gate
    )
    left, right = kernel(assemble, (array((256, 256), BF16), array((256, 256), BF16)))(exchange(sides))
    left = lax.all_gather(left, "core", axis=0, tiled=True)
    parts = kernel(multiply, array((512, 256), BF16))(left, right)
    out = kernel(finish, array((512, 128), BF16))(exchange(parts), tokens, gate, gain_mid.reshape(1, 128), w_out)
    return out.reshape(pair.shape)


def solution(mesh):
    fine = Mesh(mesh.devices.reshape(2, 8, 2, 4, 4), AXES)
    pair_spec = P(AXES[:3], AXES[3:], None)
    in_specs = (pair_spec, P(AXES[:3], AXES[3:]), P(), P(), P(), P(), P())
    return jax.shard_map(shards, mesh=fine, in_specs=in_specs, out_specs=pair_spec, check_vma=False)
```

```python
import jax
import jax.numpy as jnp
from jax import lax
from jax.experimental import pallas as pl
from jax.experimental.pallas import tpu as pltpu
from jax.sharding import Mesh
from jax.sharding import PartitionSpec as P

AXES = ("z_lo", "y", "core", "x", "z_hi")
F32, BF16 = jnp.float32, jnp.bfloat16


def iota(shape, axis):
    return lax.broadcasted_iota(jnp.int32, shape, axis)


def project(*refs):
    sources, (send_ref, gate_ref, pair_ref, gain_mid_ref, w_out_ref) = refs[:7], refs[7:12]
    mask_ref, gain_ref, w_in_ref, w_gate_ref, arrived = refs[12:]
    targets = (pair_ref, mask_ref, gain_ref, w_in_ref, w_gate_ref, gain_mid_ref, w_out_ref)
    copies = [
        pltpu.make_async_copy(source, target, arrived.at[n]) for n, (source, target) in enumerate(zip(sources, targets))
    ]
    for copy in copies:
        copy.start()
    for copy in copies:
        copy.wait()
    values = pair_ref[...].astype(F32)
    center = values - jnp.mean(values, axis=-1, keepdims=True)
    spread = jnp.mean(center * center, axis=-1, keepdims=True)
    normed = (center * lax.rsqrt(spread + 1e-05) * gain_ref[...]).astype(BF16)
    gate_ref[...] = jax.nn.sigmoid(jnp.dot(normed, w_gate_ref[...], preferred_element_type=F32))
    place = iota((32, 512), 1)
    spread_mask = jnp.dot(
        mask_ref[...].astype(F32), (place & 31 == iota((32, 512), 0)).astype(F32), preferred_element_type=F32
    )
    row = iota((16, 512), 1) >> 5
    keeper = jnp.sum(jnp.where(row == iota((16, 512), 0), spread_mask, 0.0), axis=0, keepdims=True)
    projected = lax.dot_general(w_in_ref[...], normed, (((0,), (1,)), ((), ())), preferred_element_type=F32)
    for side in range(2):
        start = side * 256
        both = (
            jax.nn.sigmoid(projected[start : start + 128]) * projected[start + 128 : start + 256] * keeper
        ).astype(BF16)
        for half in range(2):
            at = side * 1024 + half * 512
            send_ref[:, at : at + 512] = both[half * 64 : half * 64 + 64]


def turn(blocks, width):
    rows, lanes = blocks.shape
    return jnp.concatenate(
        [
            jnp.concatenate([blocks[a : a + 16, b : b + width] for a in range(0, rows, 16)], axis=1)
            for b in range(0, lanes, width)
        ],
        axis=0,
    )


def assemble(got_ref, left_ref, right_ref):
    left_ref[...] = jnp.concatenate([turn(got_ref[:, at : at + 512], 32) for at in (0, 512)], axis=1)
    right = jnp.concatenate([turn(got_ref[:, at : at + 512], 32) for at in (1024, 1536)], axis=1)
    to, source = iota((256, 256), 0), iota((256, 256), 1)
    moved = ((to & 15) * 16 + (to >> 4) == source).astype(BF16)
    right_ref[...] = jnp.dot(moved, right, preferred_element_type=F32).astype(BF16)


def multiply(left_ref, right_ref, send_ref):
    for half in range(2):
        channel = slice(half * 128, half * 128 + 128)
        summed = lax.dot_general(
            left_ref[:, channel], right_ref[:, channel], (((1,), (1,)), ((), ())), preferred_element_type=F32
        ).astype(BF16)
        for parity in range(2):
            at = half * 512 + parity * 256
            send_ref[:, at : at + 256] = turn(summed[:, parity * 256 : parity * 256 + 256], 16)


def finish(got_ref, pair_ref, gate_ref, gain_ref, w_out_ref, out_ref):
    same = iota((128, 128), 0) == iota((128, 128), 1)
    gain = jnp.sum(jnp.where(same, gain_ref[...], 0.0), axis=1, keepdims=True)
    parts = []
    for x in range(4):
        four = [got_ref[x * 64 + part * 16 : x * 64 + part * 16 + 16, :].astype(F32) for part in range(4)]
        parts.append((four[0] + four[1]) + (four[2] + four[3]))
    summed = jnp.concatenate([part[:, at : at + 512] for at in (0, 512) for part in parts], axis=0)
    center = summed - jnp.mean(summed, axis=0, keepdims=True)
    spread = jnp.mean(center * center, axis=0, keepdims=True)
    middle = (center * lax.rsqrt(spread + 1e-05) * gain).astype(BF16)
    update = lax.dot_general(middle, w_out_ref[...], (((0,), (0,)), ((), ())), preferred_element_type=F32)
    update = jnp.concatenate(
        [update[parity * 256 + i * 16 : parity * 256 + i * 16 + 16] for i in range(16) for parity in range(2)], axis=0
    )
    out_ref[...] = (pair_ref[...].astype(F32) + gate_ref[...] * update).astype(BF16)


def kernel(body, out_shape, **more):
    return pl.pallas_call(
        body, out_shape=out_shape, compiler_params=pltpu.CompilerParams(vmem_limit_bytes=32 * 1024 * 1024), **more
    )


def exchange(rows, axes):
    many, lanes = rows.shape
    return lax.all_to_all(rows.reshape(many, lanes // 128, 128), axes, 0, 0).reshape(many, lanes)


def shards(pair, pair_mask, gain_in, w_in, w_gate, gain_mid, w_out):
    array = jax.ShapeDtypeStruct
    sides, gate, tokens, gain_mid, w_out = kernel(
        project,
        (
            array((64, 2048), BF16),
            array((512, 128), F32),
            array((512, 128), BF16),
            array((1, 128), F32),
            array((128, 128), BF16),
        ),
        in_specs=[pl.BlockSpec(memory_space=pltpu.HBM)] * 7,
        scratch_shapes=[
            pltpu.VMEM((16, 32), jnp.int32),
            pltpu.VMEM((1, 128), F32),
            pltpu.VMEM((128, 512), BF16),
            pltpu.VMEM((128, 128), BF16),
            pltpu.SemaphoreType.DMA((7,)),
        ],
    )(
        *(
            pltpu.with_memory_space_constraint(value, pltpu.HBM)
            for value in (
                pair.reshape(512, 128),
                pair_mask,
                gain_in.reshape(1, 128),
                w_in,
                w_gate,
                gain_mid.reshape(1, 128),
                w_out,
            )
        )
    )
    left, right = kernel(assemble, (array((256, 256), BF16), array((256, 256), BF16)))(
        exchange(sides, ("x", "z_lo", "y"))
    )
    right = lax.all_gather(right, "core", axis=0, tiled=True)
    parts = kernel(multiply, array((256, 1024), BF16))(left, right)
    out = kernel(finish, array((512, 128), BF16))(exchange(parts, ("x", "z_hi", "z_lo", "y")), tokens, gate, gain_mid, w_out)
    return out.reshape(pair.shape)


def solution(mesh):
    fine = Mesh(mesh.devices.reshape(2, 8, 2, 4, 4), AXES)
    pair_spec = P(AXES[:3], AXES[3:], None)
    in_specs = (pair_spec, P(AXES[:3], AXES[3:]), P(), P(), P(), P(), P())
    return jax.shard_map(shards, mesh=fine, in_specs=in_specs, out_specs=pair_spec, check_vma=False)
```

```python
import jax
import jax.numpy as jnp
from jax import lax
from jax.experimental import pallas as pl
from jax.experimental.pallas import tpu as pltpu
from jax.sharding import Mesh
from jax.sharding import PartitionSpec as P

AXES = ("z_lo", "y", "core", "x", "z_out", "z_in")
F32, BF16 = jnp.float32, jnp.bfloat16


def iota(shape, axis):
    return lax.broadcasted_iota(jnp.int32, shape, axis)


def project(*refs):
    sources, (send_ref, gate_ref, pair_ref, gain_mid_ref, w_out_ref) = refs[:7], refs[7:12]
    mask_ref, gain_ref, w_in_ref, w_gate_ref, arrived = refs[12:]
    targets = (pair_ref, mask_ref, gain_ref, w_in_ref, w_gate_ref, gain_mid_ref, w_out_ref)
    copies = [
        pltpu.make_async_copy(source, target, arrived.at[n]) for n, (source, target) in enumerate(zip(sources, targets))
    ]
    for copy in copies:
        copy.start()
    copies[0].wait()
    copies[2].wait()
    values = pair_ref[...].astype(F32)
    center = values - jnp.mean(values, axis=-1, keepdims=True)
    spread = jnp.mean(center * center, axis=-1, keepdims=True)
    normed = (center * lax.rsqrt(spread + 1e-05) * gain_ref[...]).astype(BF16)
    for n in (1, 3, 4, 5, 6):
        copies[n].wait()
    gate_ref[...] = jax.nn.sigmoid(jnp.dot(normed, w_gate_ref[...], preferred_element_type=F32))
    place = iota((32, 512), 1)
    spread_mask = jnp.dot(
        mask_ref[...].astype(F32), (place & 31 == iota((32, 512), 0)).astype(F32), preferred_element_type=F32
    )
    row = iota((16, 512), 1) >> 5
    keeper = jnp.sum(jnp.where(row == iota((16, 512), 0), spread_mask, 0.0), axis=0, keepdims=True)
    projected = lax.dot_general(w_in_ref[...], normed, (((0,), (1,)), ((), ())), preferred_element_type=F32)
    for side in range(2):
        start = side * 256
        both = (
            jax.nn.sigmoid(projected[start : start + 128]) * projected[start + 128 : start + 256] * keeper
        )
        send_ref[:, side * 512 : side * 512 + 512] = both.astype(BF16)


def turn(blocks):
    rows, lanes = blocks.shape
    return jnp.concatenate(
        [
            jnp.concatenate([blocks[a : a + 16, b : b + 32] for a in range(0, rows, 16)], axis=1)
            for b in range(0, lanes, 32)
        ],
        axis=0,
    )


def assemble(got_ref, left_ref, right_ref):
    left_ref[...] = turn(got_ref[:, :512])
    to, source = iota((256, 256), 0), iota((256, 256), 1)
    moved = ((to & 15) * 16 + (to >> 4) == source).astype(BF16)
    right_ref[...] = jnp.dot(moved, turn(got_ref[:, 512:]), preferred_element_type=F32).astype(BF16)


def multiply(left_ref, right_ref, send_ref):
    right = jnp.concatenate(
        [right_ref[parity * 256 + q * 16 : parity * 256 + q * 16 + 16, :] for q in range(16) for parity in range(2)],
        axis=0,
    )
    summed = lax.dot_general(left_ref[...], right, (((1,), (1,)), ((), ())), preferred_element_type=F32)
    send_ref[...] = turn(summed.astype(BF16))


def finish(got_ref, pair_ref, gate_ref, gain_ref, w_out_ref, out_ref):
    same = iota((128, 128), 0) == iota((128, 128), 1)
    gain = jnp.sum(jnp.where(same, gain_ref[...], 0.0), axis=1, keepdims=True)
    summed = jnp.concatenate(
        [got_ref[at : at + 32, :].astype(F32) + got_ref[at + 32 : at + 64, :].astype(F32) for at in range(0, 256, 64)], axis=0
    )
    center = summed - jnp.mean(summed, axis=0, keepdims=True)
    spread = jnp.mean(center * center, axis=0, keepdims=True)
    middle = (center * lax.rsqrt(spread + 1e-05) * gain).astype(BF16)
    update = lax.dot_general(middle, w_out_ref[...], (((0,), (0,)), ((), ())), preferred_element_type=F32)
    out_ref[...] = (pair_ref[...].astype(F32) + gate_ref[...] * update).astype(BF16)


def kernel(body, out_shape, **more):
    return pl.pallas_call(
        body, out_shape=out_shape, compiler_params=pltpu.CompilerParams(vmem_limit_bytes=32 * 1024 * 1024), **more
    )


def exchange(rows, axes):
    many, lanes = rows.shape
    return lax.all_to_all(rows.reshape(many, lanes // 128, 128), axes, 0, 0).reshape(many, lanes)


def shards(pair, pair_mask, gain_in, w_in, w_gate, gain_mid, w_out):
    array = jax.ShapeDtypeStruct
    sides, gate, tokens, gain_mid, w_out = kernel(
        project,
        (
            array((128, 1024), BF16),
            array((512, 128), F32),
            array((512, 128), BF16),
            array((1, 128), F32),
            array((128, 128), BF16),
        ),
        in_specs=[pl.BlockSpec(memory_space=pltpu.HBM)] * 7,
        scratch_shapes=[
            pltpu.VMEM((16, 32), jnp.int32),
            pltpu.VMEM((1, 128), F32),
            pltpu.VMEM((128, 512), BF16),
            pltpu.VMEM((128, 128), BF16),
            pltpu.SemaphoreType.DMA((7,)),
        ],
    )(
        *(
            pltpu.with_memory_space_constraint(value, pltpu.HBM)
            for value in (
                pair.reshape(512, 128),
                pair_mask,
                gain_in.reshape(1, 128),
                w_in,
                w_gate,
                gain_mid.reshape(1, 128),
                w_out,
            )
        )
    )
    left, right = kernel(assemble, (array((256, 256), BF16), array((256, 256), BF16)))(
        exchange(sides, ("x", "z_in", "z_lo", "y"))
    )
    right = lax.all_gather(right, "core", axis=0, tiled=True)
    parts = kernel(multiply, array((256, 512), BF16))(left, right)
    out = kernel(finish, array((512, 128), BF16))(exchange(parts, ("x", "z_out", "z_in", "z_lo", "y")), tokens, gate, gain_mid, w_out)
    return out.reshape(pair.shape)


def solution(mesh):
    fine = Mesh(mesh.devices.reshape(2, 8, 2, 4, 2, 2), AXES)
    pair_spec = P(AXES[:3], AXES[3:], None)
    in_specs = (pair_spec, P(AXES[:3], AXES[3:]), P(), P(), P(), P(), P())
    return jax.shard_map(shards, mesh=fine, in_specs=in_specs, out_specs=pair_spec, check_vma=False)
```

```python
import jax
import jax.numpy as jnp
from jax import lax
from jax.experimental import pallas as pl
from jax.experimental.pallas import tpu as pltpu
from jax.sharding import Mesh
from jax.sharding import PartitionSpec as P

AXES = ("z_lo", "y", "core", "x1", "x0", "z_out", "z_in")
F32, BF16 = jnp.float32, jnp.bfloat16


def iota(shape, axis):
    return lax.broadcasted_iota(jnp.int32, shape, axis)


def project(*refs):
    sources, (send_ref, gate_ref, pair_ref, gain_mid_ref, w_out_ref) = refs[:7], refs[7:12]
    mask_ref, gain_ref, w_in_ref, w_gate_ref, arrived = refs[12:]
    targets = (pair_ref, mask_ref, gain_ref, w_in_ref, w_gate_ref, gain_mid_ref, w_out_ref)
    copies = [
        pltpu.make_async_copy(source, target, arrived.at[n]) for n, (source, target) in enumerate(zip(sources, targets))
    ]
    for copy in copies:
        copy.start()
    copies[0].wait()
    copies[2].wait()
    values = pair_ref[...].astype(F32)
    center = values - jnp.mean(values, axis=-1, keepdims=True)
    spread = jnp.mean(center * center, axis=-1, keepdims=True)
    normed = (center * lax.rsqrt(spread + 1e-05) * gain_ref[...]).astype(BF16)
    for n in (1, 3, 4, 5, 6):
        copies[n].wait()
    gate_ref[...] = jax.nn.sigmoid(jnp.dot(normed, w_gate_ref[...], preferred_element_type=F32))
    place = iota((32, 512), 1)
    spread_mask = jnp.dot(
        mask_ref[...].astype(F32), (place & 31 == iota((32, 512), 0)).astype(F32), preferred_element_type=F32
    )
    row = iota((16, 512), 1) >> 5
    keeper = jnp.sum(jnp.where(row == iota((16, 512), 0), spread_mask, 0.0), axis=0, keepdims=True)
    projected = lax.dot_general(w_in_ref[...], normed, (((0,), (1,)), ((), ())), preferred_element_type=F32)
    for side in range(2):
        start = side * 256
        both = (
            jax.nn.sigmoid(projected[start : start + 128]) * projected[start + 128 : start + 256] * keeper
        )
        send_ref[:, side * 512 : side * 512 + 512] = both.astype(BF16)


def turn(blocks):
    rows, lanes = blocks.shape
    return jnp.concatenate(
        [
            jnp.concatenate([blocks[a : a + 16, b : b + 32] for a in range(0, rows, 16)], axis=1)
            for b in range(0, lanes, 32)
        ],
        axis=0,
    )


def assemble(got_ref, left_ref, right_ref):
    left_ref[...] = turn(got_ref[:, :512])
    to, source = iota((256, 256), 0), iota((256, 256), 1)
    moved = ((to & 15) * 16 + (to >> 4) == source).astype(BF16)
    right_ref[...] = jnp.dot(moved, turn(got_ref[:, 512:]), preferred_element_type=F32).astype(BF16)


def multiply(left_ref, right_ref, send_ref):
    right = jnp.concatenate(
        [
            right_ref[parity * 256 + q * 16 : parity * 256 + q * 16 + 16, :]
            for q in (x1 * 8 + x0 * 4 + z for x0 in range(2) for out in range(2) for x1 in range(2) for z in (out * 2, out * 2 + 1))
            for parity in range(2)
        ],
        axis=0,
    )
    summed = lax.dot_general(left_ref[...], right, (((1,), (1,)), ((), ())), preferred_element_type=F32)
    send_ref[...] = turn(summed.astype(BF16))


def finish(got_ref, pair_ref, gate_ref, gain_ref, w_out_ref, out_ref):
    same = iota((128, 128), 0) == iota((128, 128), 1)
    gain = jnp.sum(jnp.where(same, gain_ref[...], 0.0), axis=1, keepdims=True)
    summed = jnp.concatenate(
        [
            got_ref[at : at + 32, :].astype(F32) + got_ref[at + 64 : at + 96, :].astype(F32)
            for at in (x0 * 128 + x1 * 32 for x1 in range(2) for x0 in range(2))
        ],
        axis=0,
    )
    center = summed - jnp.mean(summed, axis=0, keepdims=True)
    spread = jnp.mean(center * center, axis=0, keepdims=True)
    middle = (center * lax.rsqrt(spread + 1e-05) * gain).astype(BF16)
    update = lax.dot_general(middle, w_out_ref[...], (((0,), (0,)), ((), ())), preferred_element_type=F32)
    out_ref[...] = (pair_ref[...].astype(F32) + gate_ref[...] * update).astype(BF16)


def kernel(body, out_shape, **more):
    return pl.pallas_call(
        body, out_shape=out_shape, compiler_params=pltpu.CompilerParams(vmem_limit_bytes=32 * 1024 * 1024), **more
    )


def exchange(rows, axes):
    many, lanes = rows.shape
    return lax.all_to_all(rows.reshape(many, lanes // 128, 128), axes, 0, 0).reshape(many, lanes)


def shards(pair, pair_mask, gain_in, w_in, w_gate, gain_mid, w_out):
    array = jax.ShapeDtypeStruct
    sides, gate, tokens, gain_mid, w_out = kernel(
        project,
        (
            array((128, 1024), BF16),
            array((512, 128), F32),
            array((512, 128), BF16),
            array((1, 128), F32),
            array((128, 128), BF16),
        ),
        in_specs=[pl.BlockSpec(memory_space=pltpu.HBM)] * 7,
        scratch_shapes=[
            pltpu.VMEM((16, 32), jnp.int32),
            pltpu.VMEM((1, 128), F32),
            pltpu.VMEM((128, 512), BF16),
            pltpu.VMEM((128, 128), BF16),
            pltpu.SemaphoreType.DMA((7,)),
        ],
    )(
        *(
            pltpu.with_memory_space_constraint(value, pltpu.HBM)
            for value in (
                pair.reshape(512, 128),
                pair_mask,
                gain_in.reshape(1, 128),
                w_in,
                w_gate,
                gain_mid.reshape(1, 128),
                w_out,
            )
        )
    )
    left, right = kernel(assemble, (array((256, 256), BF16), array((256, 256), BF16)))(
        exchange(sides, ("x1", "x0", "z_in", "z_lo", "y"))
    )
    right = lax.all_gather(right, "core", axis=0, tiled=True)
    parts = kernel(multiply, array((256, 512), BF16))(left, right)
    out = kernel(finish, array((512, 128), BF16))(exchange(parts, ("x0", "z_out", "x1", "z_in", "z_lo", "y")), tokens, gate, gain_mid, w_out)
    return out.reshape(pair.shape)


def solution(mesh):
    fine = Mesh(mesh.devices.reshape(2, 8, 2, 2, 2, 2, 2), AXES)
    pair_spec = P(AXES[:3], AXES[3:], None)
    in_specs = (pair_spec, P(AXES[:3], AXES[3:]), P(), P(), P(), P(), P())
    return jax.shard_map(shards, mesh=fine, in_specs=in_specs, out_specs=pair_spec, check_vma=False)
```

```python
import jax
import jax.numpy as jnp
from jax import lax
from jax.experimental import pallas as pl
from jax.experimental.pallas import tpu as pltpu
from jax.sharding import Mesh
from jax.sharding import PartitionSpec as P

AXES = ("z_lo", "y", "core", "x1", "x0", "z_out", "z_in")
F32, BF16 = jnp.float32, jnp.bfloat16


def sigmoid(values):
    return 0.5 * jnp.tanh(0.5 * values) + 0.5


def iota(shape, axis):
    return lax.broadcasted_iota(jnp.int32, shape, axis)


def project(*refs):
    sources, (send_ref, gate_ref, pair_ref, gain_mid_ref, w_out_ref) = refs[:7], refs[7:12]
    mask_ref, gain_ref, w_in_ref, w_gate_ref, arrived = refs[12:]
    targets = (pair_ref, mask_ref, gain_ref, w_in_ref, w_gate_ref, gain_mid_ref, w_out_ref)
    copies = [
        pltpu.make_async_copy(source, target, arrived.at[n]) for n, (source, target) in enumerate(zip(sources, targets))
    ]
    for copy in copies:
        copy.start()
    copies[0].wait()
    copies[2].wait()
    values = pair_ref[...].astype(F32)
    center = values - jnp.mean(values, axis=-1, keepdims=True)
    spread = jnp.mean(center * center, axis=-1, keepdims=True)
    normed = (center * lax.rsqrt(spread + 1e-05) * gain_ref[...]).astype(BF16)
    for n in (1, 3, 4, 5, 6):
        copies[n].wait()
    gate_ref[...] = sigmoid(jnp.dot(normed, w_gate_ref[...], preferred_element_type=F32))
    place = iota((32, 512), 1)
    spread_mask = jnp.dot(
        mask_ref[...].astype(F32), (place & 31 == iota((32, 512), 0)).astype(F32), preferred_element_type=F32
    )
    row = iota((16, 512), 1) >> 5
    keeper = jnp.sum(jnp.where(row == iota((16, 512), 0), spread_mask, 0.0), axis=0, keepdims=True)
    projected = lax.dot_general(w_in_ref[...], normed, (((0,), (1,)), ((), ())), preferred_element_type=F32)
    for side in range(2):
        start = side * 256
        both = (
            sigmoid(projected[start : start + 128]) * projected[start + 128 : start + 256] * keeper
        )
        send_ref[:, side * 512 : side * 512 + 512] = both.astype(BF16)


def turn(blocks):
    rows, lanes = blocks.shape
    return jnp.concatenate(
        [
            jnp.concatenate([blocks[a : a + 16, b : b + 32] for a in range(0, rows, 16)], axis=1)
            for b in range(0, lanes, 32)
        ],
        axis=0,
    )


def assemble(got_ref, left_ref, right_ref):
    left_ref[...] = turn(got_ref[:, :512])
    to, source = iota((256, 256), 0), iota((256, 256), 1)
    moved = ((to & 15) * 16 + (to >> 4) == source).astype(BF16)
    right_ref[...] = jnp.dot(moved, turn(got_ref[:, 512:]), preferred_element_type=F32).astype(BF16)


def multiply(left_ref, right_ref, send_ref):
    right = jnp.concatenate(
        [
            right_ref[parity * 256 + q * 16 : parity * 256 + q * 16 + 16, :]
            for q in (x1 * 8 + x0 * 4 + z for x0 in range(2) for out in range(2) for x1 in range(2) for z in (out * 2, out * 2 + 1))
            for parity in range(2)
        ],
        axis=0,
    )
    summed = lax.dot_general(left_ref[...], right, (((1,), (1,)), ((), ())), preferred_element_type=F32)
    send_ref[...] = turn(summed.astype(BF16))


def finish(got_ref, pair_ref, gate_ref, gain_ref, w_out_ref, out_ref):
    same = iota((128, 128), 0) == iota((128, 128), 1)
    gain = jnp.sum(jnp.where(same, gain_ref[...], 0.0), axis=1, keepdims=True)
    summed = jnp.concatenate(
        [
            got_ref[at : at + 32, :].astype(F32) + got_ref[at + 64 : at + 96, :].astype(F32)
            for at in (x0 * 128 + x1 * 32 for x1 in range(2) for x0 in range(2))
        ],
        axis=0,
    )
    center = summed - jnp.mean(summed, axis=0, keepdims=True)
    spread = jnp.mean(center * center, axis=0, keepdims=True)
    middle = (center * lax.rsqrt(spread + 1e-05) * gain).astype(BF16)
    update = lax.dot_general(middle, w_out_ref[...], (((0,), (0,)), ((), ())), preferred_element_type=F32)
    out_ref[...] = (pair_ref[...].astype(F32) + gate_ref[...] * update).astype(BF16)


def kernel(body, out_shape, **more):
    return pl.pallas_call(
        body, out_shape=out_shape, compiler_params=pltpu.CompilerParams(vmem_limit_bytes=32 * 1024 * 1024), **more
    )


def exchange(rows, axes):
    many, lanes = rows.shape
    return lax.all_to_all(rows.reshape(many, lanes // 128, 128), axes, 0, 0).reshape(many, lanes)


def shards(pair, pair_mask, gain_in, w_in, w_gate, gain_mid, w_out):
    array = jax.ShapeDtypeStruct
    sides, gate, tokens, gain_mid, w_out = kernel(
        project,
        (
            array((128, 1024), BF16),
            array((512, 128), F32),
            array((512, 128), BF16),
            array((1, 128), F32),
            array((128, 128), BF16),
        ),
        in_specs=[pl.BlockSpec(memory_space=pltpu.HBM)] * 7,
        scratch_shapes=[
            pltpu.VMEM((16, 32), jnp.int32),
            pltpu.VMEM((1, 128), F32),
            pltpu.VMEM((128, 512), BF16),
            pltpu.VMEM((128, 128), BF16),
            pltpu.SemaphoreType.DMA((7,)),
        ],
    )(
        *(
            pltpu.with_memory_space_constraint(value, pltpu.HBM)
            for value in (
                pair.reshape(512, 128),
                pair_mask,
                gain_in.reshape(1, 128),
                w_in,
                w_gate,
                gain_mid.reshape(1, 128),
                w_out,
            )
        )
    )
    left, right = kernel(assemble, (array((256, 256), BF16), array((256, 256), BF16)))(
        exchange(sides, ("x1", "x0", "z_in", "z_lo", "y"))
    )
    right = lax.all_gather(right, "core", axis=0, tiled=True)
    parts = kernel(multiply, array((256, 512), BF16))(left, right)
    out = kernel(finish, array((512, 128), BF16))(exchange(parts, ("x0", "z_out", "x1", "z_in", "z_lo", "y")), tokens, gate, gain_mid, w_out)
    return out.reshape(pair.shape)


def solution(mesh):
    fine = Mesh(mesh.devices.reshape(2, 8, 2, 2, 2, 2, 2), AXES)
    pair_spec = P(AXES[:3], AXES[3:], None)
    in_specs = (pair_spec, P(AXES[:3], AXES[3:]), P(), P(), P(), P(), P())
    return jax.shard_map(shards, mesh=fine, in_specs=in_specs, out_specs=pair_spec, check_vma=False)
```

```python
import jax
import jax.numpy as jnp
from jax import lax
from jax.experimental import pallas as pl
from jax.experimental.pallas import tpu as pltpu
from jax.sharding import Mesh
from jax.sharding import PartitionSpec as P

AXES = ("z_lo", "y", "core", "x1", "x0", "z_out", "z_in")
F32, BF16 = jnp.float32, jnp.bfloat16


def sigmoid(values):
    return 0.5 * jnp.tanh(0.5 * values) + 0.5


def iota(shape, axis):
    return lax.broadcasted_iota(jnp.int32, shape, axis)


def project(*refs):
    sources, (send_ref, gate_ref, pair_ref, gain_mid_ref, w_out_ref) = refs[:7], refs[7:12]
    mask_ref, gain_ref, w_in_ref, w_gate_ref, arrived = refs[12:]
    targets = (pair_ref, mask_ref, gain_ref, w_in_ref, w_gate_ref, gain_mid_ref, w_out_ref)
    copies = [
        pltpu.make_async_copy(source, target, arrived.at[n]) for n, (source, target) in enumerate(zip(sources, targets))
    ]
    for copy in copies:
        copy.start()
    copies[0].wait()
    copies[2].wait()
    values = pair_ref[...].astype(F32)
    center = values - jnp.mean(values, axis=-1, keepdims=True)
    spread = jnp.mean(center * center, axis=-1, keepdims=True)
    normed = (center * lax.rsqrt(spread + 1e-05) * gain_ref[...]).astype(BF16)
    for n in (1, 3, 4, 5, 6):
        copies[n].wait()
    gate_ref[...] = sigmoid(jnp.dot(normed, w_gate_ref[...], preferred_element_type=F32))
    place = iota((32, 512), 1)
    spread_mask = jnp.dot(
        mask_ref[...].astype(F32), (place & 31 == iota((32, 512), 0)).astype(F32), preferred_element_type=F32
    )
    row = iota((16, 512), 1) >> 5
    keeper = jnp.sum(jnp.where(row == iota((16, 512), 0), spread_mask, 0.0), axis=0, keepdims=True)
    projected = lax.dot_general(w_in_ref[...], normed, (((0,), (1,)), ((), ())), preferred_element_type=F32)
    for side in range(2):
        start = side * 256
        both = (
            sigmoid(projected[start : start + 128]) * projected[start + 128 : start + 256] * keeper
        )
        send_ref[:, side * 512 : side * 512 + 512] = both.astype(BF16)


def turn(blocks):
    rows, lanes = blocks.shape
    return jnp.concatenate(
        [
            jnp.concatenate([blocks[a : a + 16, b : b + 32] for a in range(0, rows, 16)], axis=1)
            for b in range(0, lanes, 32)
        ],
        axis=0,
    )


def assemble(got_ref, left_ref, right_ref):
    left_ref[...] = turn(got_ref[:, :512])
    to, source = iota((256, 256), 0), iota((256, 256), 1)
    moved = ((to & 15) * 16 + (to >> 4) == source).astype(BF16)
    right_ref[...] = jnp.dot(moved, turn(got_ref[:, 512:]), preferred_element_type=F32).astype(BF16)


def multiply(left_ref, right_ref, send_ref):
    right = jnp.concatenate(
        [
            right_ref[parity * 256 + q * 16 : parity * 256 + q * 16 + 16, :]
            for q in (x1 * 8 + x0 * 4 + z for x0 in range(2) for out in range(2) for x1 in range(2) for z in (out * 2, out * 2 + 1))
            for parity in range(2)
        ],
        axis=0,
    )
    summed = lax.dot_general(left_ref[...], right, (((1,), (1,)), ((), ())), preferred_element_type=F32)
    send_ref[...] = turn(summed.astype(BF16))


def finish(got_ref, pair_ref, gate_ref, gain_ref, w_out_ref, out_ref):
    same = iota((128, 128), 0) == iota((128, 128), 1)
    gain = jnp.sum(jnp.where(same, gain_ref[...], 0.0), axis=1, keepdims=True)
    summed = jnp.concatenate(
        [
            got_ref[at : at + 16, :].astype(F32) + got_ref[at + 64 : at + 80, :].astype(F32)
            for at in (x0 * 128 + x1 * 32 + z_in * 16 for z_in in range(2) for x1 in range(2) for x0 in range(2))
        ],
        axis=0,
    )
    center = summed - jnp.mean(summed, axis=0, keepdims=True)
    spread = jnp.mean(center * center, axis=0, keepdims=True)
    middle = (center * lax.rsqrt(spread + 1e-05) * gain).astype(BF16)
    update = lax.dot_general(middle, w_out_ref[...], (((0,), (0,)), ((), ())), preferred_element_type=F32)
    out_ref[...] = (pair_ref[...].astype(F32) + gate_ref[...] * update).astype(BF16)


def kernel(body, out_shape, **more):
    return pl.pallas_call(
        body, out_shape=out_shape, compiler_params=pltpu.CompilerParams(vmem_limit_bytes=32 * 1024 * 1024), **more
    )


def exchange(rows, axes):
    many, lanes = rows.shape
    return lax.all_to_all(rows.reshape(many, lanes // 128, 128), axes, 0, 0).reshape(many, lanes)


def shards(pair, pair_mask, gain_in, w_in, w_gate, gain_mid, w_out):
    array = jax.ShapeDtypeStruct
    sides, gate, tokens, gain_mid, w_out = kernel(
        project,
        (
            array((128, 1024), BF16),
            array((512, 128), F32),
            array((512, 128), BF16),
            array((1, 128), F32),
            array((128, 128), BF16),
        ),
        in_specs=[pl.BlockSpec(memory_space=pltpu.HBM)] * 7,
        scratch_shapes=[
            pltpu.VMEM((16, 32), jnp.int32),
            pltpu.VMEM((1, 128), F32),
            pltpu.VMEM((128, 512), BF16),
            pltpu.VMEM((128, 128), BF16),
            pltpu.SemaphoreType.DMA((7,)),
        ],
    )(
        *(
            pltpu.with_memory_space_constraint(value, pltpu.HBM)
            for value in (
                pair.reshape(512, 128),
                pair_mask,
                gain_in.reshape(1, 128),
                w_in,
                w_gate,
                gain_mid.reshape(1, 128),
                w_out,
            )
        )
    )
    left, right = kernel(assemble, (array((256, 256), BF16), array((256, 256), BF16)))(
        exchange(sides, ("z_in", "x1", "x0", "z_lo", "y"))
    )
    right = lax.all_gather(right, "core", axis=0, tiled=True)
    parts = kernel(multiply, array((256, 512), BF16))(left, right)
    out = kernel(finish, array((512, 128), BF16))(exchange(parts, ("x0", "z_out", "x1", "z_in", "z_lo", "y")), tokens, gate, gain_mid, w_out)
    return out.reshape(pair.shape)


def solution(mesh):
    fine = Mesh(mesh.devices.reshape(2, 8, 2, 2, 2, 2, 2), AXES)
    pair_spec = P(AXES[:3], AXES[3:], None)
    in_specs = (pair_spec, P(AXES[:3], AXES[3:]), P(), P(), P(), P(), P())
    return jax.shard_map(shards, mesh=fine, in_specs=in_specs, out_specs=pair_spec, check_vma=False)
```
